256 devices in a mesh: dp: 16 (over z_lo, x, core), ctx: 16 (over y, z_hi).
Axes of the slice: x: 4, y: 4, z: 8 (z_hi: 4, z_lo: 2; z = z_hi * 2 + z_lo), core: 2. Of those that a mesh axis runs over, the one named last changes fastest.
Arguments:
- queries: bfloat16 [131072, 32, 128], P(('dp', 'ctx')), may hold values from -8 to 8
- keys: bfloat16 [131072, 4, 128], P(('dp', 'ctx')), may hold values from -8 to 8
- values: bfloat16 [131072, 4, 128], P(('dp', 'ctx')), may hold values from -6 to 6
- doc_lengths: int32 [16, 16], P('dp'), may hold values from 1 to 1024, 8192 in all within a row
Outputs:
- attended: bfloat16 [131072, 32, 128], P(('dp', 'ctx'))
The draws below stay inside these ranges and needn't reach their ends.
All inputs are finite; a program needn't handle non-finite values.
Results may differ from the reference program's by a relative error of at most 0.0035.
Values may be sent and summed in bfloat16 or wider, within the bound.
No kernel may reach another device: no remote copies, remote signals or barrier semaphores. Data moves between devices by JAX's collectives and lax.ppermute only.
A program may use at most 128 MiB of HBM per device.

```python
import math
import jax
import jax.numpy as jnp
import numpy as np
from jax import lax

QUERY_HEADS = 32
KEY_VALUE_HEADS = 4
HEAD_DIMENSION = 128
TILE_TOKENS = 512
SEQ = 8192
TOKEN_TOTAL = 131072
DOCS = 16
DOC_MOST = 1024
N_DP = 16
N_CTX = 16


def drawn_pair(key):
    queries = jnp.clip(jax.random.normal(jax.random.fold_in(key, 11), (TOKEN_TOTAL, QUERY_HEADS, HEAD_DIMENSION), jnp.float32), -4.0, 4.0)
    keys = jnp.clip(jax.random.normal(jax.random.fold_in(key, 12), (TOKEN_TOTAL, KEY_VALUE_HEADS, HEAD_DIMENSION), jnp.float32), -4.0, 4.0)
    return (queries, keys)


def draw_queries(key, part):
    return drawn_pair(key)[0].astype(jnp.bfloat16)


def draw_keys(key, part):
    return drawn_pair(key)[1].astype(jnp.bfloat16)


def level_of(own_key, extent, shards, least, top_value):
    gain, own = 1.0, jax.random.fold_in(own_key, 6)
    for axis_at, shards_of in shards:
        draws = jnp.exp(jax.random.uniform(jax.random.fold_in(own, axis_at), (shards_of,), jnp.float32, least / len(shards), top_value / len(shards)))
        gain = gain * jnp.repeat(draws, extent[axis_at] // shards_of).reshape([-1 if axis == axis_at else 1 for axis in range(len(extent))])
    return gain


def length_profile(count, total, most, lean):
    weights = [(1 << 20) // math.isqrt(rank ** lean) + 1 for rank in range(2, count + 1)]
    surplus, holding = total - most - (count - 1), [1] * (count - 1)
    while surplus > 0:
        free = [i for i in range(count - 1) if holding[i] < most]
        whole, remaining = sum([weights[i] for i in free]), surplus
        for i in free:
            more = min(most - holding[i], max(1, remaining * weights[i] // whole), surplus)
            holding[i] = holding[i] + more
            surplus = surplus - more
    return np.array([most] + holding)


def uneven_parts(key, amount, total, limit, slope):
    if amount == 2:
        one = jax.random.randint(key, (), max(1, total - limit), min(limit, total - 1) + 1)
        return jnp.stack([one, total - one])
    tallies = jnp.asarray(length_profile(amount, total, limit, slope), jnp.int32)
    pairs = (amount - 1) // 2
    giver, sink = tallies[1:1 + 2 * pairs:2], tallies[2:2 + 2 * pairs:2]
    room = jnp.minimum(giver - 1, limit - sink)
    moved = jax.random.randint(jax.random.fold_in(key, 1), (pairs,), 0, 1 << 20) % (room + 1)
    tallies = tallies.at[1:1 + 2 * pairs:2].set(giver - moved).at[2:2 + 2 * pairs:2].set(sink + moved)
    return tallies[jax.random.permutation(jax.random.fold_in(key, 2), amount)]


def centred(own_key, dims, scale, bound, shards=(), held_as=jnp.bfloat16):
    entries = jax.random.normal(own_key, dims, jnp.float32) * scale
    if len(shards) > 0:
        entries = level_of(own_key, dims, shards, -0.22, 0.18) * entries
    return jnp.clip(entries, min=-bound, max=bound).astype(held_as)


def setup_inputs(seed: int = 0) -> dict:
    seeds = jax.random.split(jax.random.key(seed), 5)
    queries = draw_queries(jax.random.fold_in(seeds[4], 71), 0)
    keys = draw_keys(jax.random.fold_in(seeds[4], 71), 0)
    values = centred(seeds[2], (TOKEN_TOTAL, KEY_VALUE_HEADS, HEAD_DIMENSION), 1.0, 6.0, ((0, 256),))
    doc_lengths = jax.vmap(lambda own: uneven_parts(own, DOCS, SEQ, DOC_MOST, 2))(jax.random.split(seeds[3], N_DP)).reshape((N_DP, DOCS)).astype(jnp.int32)
    return dict(queries=queries, keys=keys, values=values, doc_lengths=doc_lengths)


def doc_index(positions, lengths):
    doc_ends = jnp.cumsum(lengths)
    return lax.optimization_barrier(jnp.sum((positions[:, None] >= doc_ends[None, :]).astype(jnp.int32), axis=1))

def tile_partial(tile_queries, block_keys, block_values, query_pos, key_pos, lengths):
    tile_rows, head_count, head_width = tile_queries.shape
    kv_count = block_keys.shape[1]
    group_size = head_count // kv_count
    allowed = doc_index(query_pos, lengths)[:, None] == doc_index(key_pos, lengths)[None, :]
    allowed = allowed & (key_pos[None, :] <= query_pos[:, None]) & (key_pos[None, :] >= 0)
    score_scale = 1.0 / math.sqrt(head_width)
    grouped = tile_queries.reshape(tile_rows, kv_count, group_size, head_width).transpose(1, 0, 2, 3)
    key_heads = block_keys.transpose(1, 0, 2)
    value_heads = block_values.transpose(1, 0, 2)

    def one_head(operands):
        query_group, key_head, value_head = operands
        scores = jnp.einsum('tgd,ud->gtu', query_group.astype(jnp.float32), key_head.astype(jnp.float32)) * score_scale
        masked = jnp.where(allowed[None], scores, -1e+30)
        maxima = lax.optimization_barrier(jnp.max(masked, axis=-1))
        weights = jnp.where(allowed[None], jnp.exp(masked - maxima[..., None]), 0.0)
        sums = lax.optimization_barrier(jnp.sum(weights, axis=-1))
        rounded = weights.astype(jnp.bfloat16)
        outputs = jnp.einsum('gtu,ud->tgd', rounded.astype(jnp.float32), value_head.astype(jnp.float32))
        return (maxima, sums, outputs)
    maxima, sums, outputs = lax.map(one_head, (grouped, key_heads, value_heads))
    maxima = maxima.reshape(head_count, tile_rows)
    sums = sums.reshape(head_count, tile_rows)
    outputs = outputs.transpose(1, 0, 2, 3).reshape(tile_rows, head_count, head_width)
    return (maxima, sums, outputs)

def merge_tiles(partials):
    row_max = partials[0][0]
    for part_item in partials[1:]:
        row_max = jnp.maximum(row_max, part_item[0])
    denominator = 0.0
    weighted = 0.0
    for maxima, sums, outputs in partials:
        factor = jnp.exp(maxima - row_max)
        denominator = denominator + factor * sums
        weighted = weighted + factor.T[:, :, None] * outputs
    return (weighted / denominator.T[:, :, None]).astype(jnp.bfloat16)

def reference(queries, keys, values, doc_lengths):
    sequence_length = TILE_TOKENS * N_CTX
    key_padding = jnp.pad(keys.reshape(N_DP, sequence_length, KEY_VALUE_HEADS, HEAD_DIMENSION), ((0, 0), (2 * TILE_TOKENS, 0), (0, 0), (0, 0)))
    value_padding = jnp.pad(values.reshape(N_DP, sequence_length, KEY_VALUE_HEADS, HEAD_DIMENSION), ((0, 0), (2 * TILE_TOKENS, 0), (0, 0), (0, 0)))

    def one_tile(tile_index):
        batch_position = (tile_index // N_CTX).astype(jnp.int32)
        shard_index = (tile_index % N_CTX).astype(jnp.int32)
        tile_queries = lax.dynamic_slice_in_dim(queries, (tile_index * TILE_TOKENS).astype(jnp.int32), TILE_TOKENS, 0)
        lengths = lax.dynamic_index_in_dim(doc_lengths, batch_position, 0, False)
        query_pos = shard_index * TILE_TOKENS + jnp.arange(TILE_TOKENS, dtype=jnp.int32)
        partials = []
        for offset in (0, 1, 2):
            start_offset = ((shard_index + 2 - offset) * TILE_TOKENS).astype(jnp.int32)
            zero_value = jnp.zeros((), jnp.int32)
            block_keys = lax.dynamic_slice(key_padding, (batch_position, start_offset, zero_value, zero_value), (1, TILE_TOKENS, KEY_VALUE_HEADS, HEAD_DIMENSION))[0]
            block_values = lax.dynamic_slice(value_padding, (batch_position, start_offset, zero_value, zero_value), (1, TILE_TOKENS, KEY_VALUE_HEADS, HEAD_DIMENSION))[0]
            partials.append(tile_partial(tile_queries, block_keys, block_values, query_pos, query_pos - offset * TILE_TOKENS, lengths))
        return merge_tiles(partials)
    attended = lax.map(one_tile, jnp.arange(N_DP * N_CTX, dtype=jnp.int32))
    return attended.reshape(TOKEN_TOTAL, QUERY_HEADS, HEAD_DIMENSION)
```

```python
import functools
import math

import jax
import jax.numpy as jnp
from jax import lax
from jax.experimental import pallas as pl
from jax.experimental.pallas import tpu as pltpu
from jax.sharding import PartitionSpec as P

CHUNK = 128
SUB = 32
PAIR = 16
FORWARD = 176
NEG = -1e30


def attend(query_group, key_part, value_part, bias, scale):
    scores = lax.dot_general(
        query_group, key_part, (((1,), (1,)), ((), ())), preferred_element_type=jnp.float32
    )
    rows, width = scores.shape
    if bias is not None:
        scores = (scores.reshape(rows // 8, 8, width) + bias).reshape(rows, width)
    maxima = jnp.max(scores, axis=-1, keepdims=True)
    weights = jnp.exp2((scores - maxima) * scale).astype(jnp.bfloat16)
    both = jnp.dot(weights, value_part, preferred_element_type=jnp.float32)
    return maxima, both[:, 128:], both[:, :128]


def pack_stats(maxima, sums):
    lane = lax.broadcasted_iota(jnp.int32, sums.shape, 1)
    return jnp.where(lane < 64, jnp.broadcast_to(maxima, sums.shape), sums)


def stage_heads(pieces, key_store, value_store, pair):
    for half in range(2):
        at = 0
        for piece in pieces:
            count = piece.shape[0]
            key_at = pl.multiple_of((pair * 2 + half) * 128, 128)
            value_at = pl.multiple_of(512 + (pair * 2 + half) * 128, 128)
            key_store[half, at : at + count, :] = piece[:, pl.ds(key_at, 128)]
            value_store[half, at : at + count, :128] = piece[:, pl.ds(value_at, 128)]
            value_store[half, at : at + count, 128:] = jnp.ones((count, 128), jnp.bfloat16)
            at += count


def group_rows(ref, rows, half):
    block = ref[rows, :, :].astype(jnp.float32)
    return block[:, half * 8 : half * 8 + 8, :].reshape(-1, 128)


def ungroup(parts):
    return jnp.concatenate([part.reshape(-1, 8, 128) for part in parts], axis=1)


def own_kernel(scale, q_ref, bias_ref, kv_ref, out_ref, sum_ref, stat_ref, key_store, value_store):
    pair = pl.program_id(0)

    @pl.when(pl.program_id(1) == 0)
    def _():
        stage_heads([kv_ref], key_store, value_store, pair)

    for step in range(CHUNK // SUB):
        rows = slice(step * SUB, (step + 1) * SUB)
        outs, sums, stats = [], [], []
        for half in range(2):
            group = group_rows(q_ref, rows, half).astype(jnp.bfloat16)
            maxima, total, output = attend(
                group, key_store[half], value_store[half], bias_ref[rows, :, :], scale
            )
            outs.append(output / total)
            sums.append(output)
            stats.append(pack_stats(maxima, total))
        out_ref[rows, :, :] = ungroup(outs).astype(jnp.bfloat16)
        sum_ref[rows, :, :] = ungroup(sums)
        stat_ref[rows, :, :] = ungroup(stats)


def back_kernel(scale, count, keep, facts, q_ref, old_out, old_sum, old_stat, *refs):
    pieces = refs[:count]
    out_ref = refs[count]
    sum_ref, stat_ref = refs[count + 1 : count + 3] if keep else (None, None)
    key_store, value_store = refs[-2:]
    pair, chunk = pl.program_id(0), pl.program_id(1)
    row_limit, key_low = facts[0], facts[1]

    @pl.when((chunk == 0) & (row_limit > 0))
    def _():
        stage_heads(pieces, key_store, value_store, pair)

    def work(rows, first_row, low):
        width = 512 - low
        position = lax.broadcasted_iota(jnp.int32, (1, 1, width), 2) + low
        bias = jnp.where(position >= key_low, 0.0, NEG).astype(jnp.float32)
        outs, sums, stats = [], [], []
        for half in range(2):
            group = group_rows(q_ref, rows, half).astype(jnp.bfloat16)
            maxima, total, output = attend(
                group, key_store[half, low:, :], value_store[half, low:, :], bias, scale
            )
            token = first_row + lax.broadcasted_iota(jnp.int32, (SUB, 8, 1), 0)
            maxima = jnp.where((token < row_limit).reshape(-1, 1), maxima, NEG)
            before = group_rows(old_sum, rows, half)
            stat = group_rows(old_stat, rows, half)
            old_max, old_total = stat[:, :1], stat[:, 64:65]
            top = jnp.maximum(old_max, maxima)
            keep_part = jnp.exp2((old_max - top) * scale)
            new_part = jnp.exp2((maxima - top) * scale)
            merged = keep_part * before + new_part * output
            total = keep_part * old_total + new_part * total
            outs.append(merged / total)
            if keep:
                sums.append(merged)
                stats.append(pack_stats(top, total))
        out_ref[rows, :, :] = ungroup(outs).astype(jnp.bfloat16)
        if keep:
            sum_ref[rows, :, :] = ungroup(sums)
            stat_ref[rows, :, :] = ungroup(stats)

    for step in range(CHUNK // SUB):
        rows = slice(step * SUB, (step + 1) * SUB)
        first_row = chunk * CHUNK + step * SUB
        active = first_row < row_limit

        @pl.when(active & (key_low < 256))
        def _():
            work(rows, first_row, 0)

        @pl.when(active & (key_low >= 256))
        def _():
            work(rows, first_row, 256)

        @pl.when(jnp.logical_not(active) & ((chunk * CHUNK < row_limit) | (chunk == 0)))
        def _():
            out_ref[rows, :, :] = old_out[rows, :, :]
            if keep:
                sum_ref[rows, :, :] = old_sum[rows, :, :]
                stat_ref[rows, :, :] = old_stat[rows, :, :]


SHAPE = (512, 32, 128)
BLOCK = (CHUNK, PAIR, 128)


def stores():
    return [
        pltpu.VMEM((2, 512, 128), jnp.bfloat16),
        pltpu.VMEM((2, 512, 256), jnp.bfloat16),
    ]


def estimate(part):
    return pl.CostEstimate(
        flops=int(part * 8.6e9), bytes_accessed=int(part * 24e6), transcendentals=int(part * 8.4e6)
    )


def own_tile(queries, bias, kv, scale):
    at = lambda pair, chunk: (chunk, pair, 0)
    return pl.pallas_call(
        functools.partial(own_kernel, scale),
        grid=(2, 512 // CHUNK),
        in_specs=[
            pl.BlockSpec(BLOCK, at),
            pl.BlockSpec((CHUNK, 1, 512), lambda pair, chunk: (chunk, 0, 0)),
            pl.BlockSpec((512, 1024), lambda pair, chunk: (0, 0)),
        ],
        out_specs=[pl.BlockSpec(BLOCK, at)] * 3,
        out_shape=[
            jax.ShapeDtypeStruct(SHAPE, jnp.bfloat16),
            jax.ShapeDtypeStruct(SHAPE, jnp.float32),
            jax.ShapeDtypeStruct(SHAPE, jnp.float32),
        ],
        scratch_shapes=stores(),
        compiler_params=pltpu.CompilerParams(vmem_limit_bytes=48 << 20),
        cost_estimate=estimate(1.0),
        name="own_tile",
    )(queries, bias, kv)


def back_tile(facts, queries, out, sums, stats, pieces, scale, keep, name):
    def at(pair, chunk, facts):
        last = jnp.maximum((facts[0] + CHUNK - 1) // CHUNK - 1, 0)
        return (jnp.minimum(chunk, last), pair, 0)

    whole = lambda pair, chunk, facts: (0, 0)
    wide = [jax.ShapeDtypeStruct(SHAPE, jnp.float32)] * 2 if keep else []
    spec = pl.BlockSpec(BLOCK, at)
    made = pl.pallas_call(
        functools.partial(back_kernel, scale, len(pieces), keep),
        grid_spec=pltpu.PrefetchScalarGridSpec(
            num_scalar_prefetch=1,
            grid=(2, 512 // CHUNK),
            in_specs=[spec] * 4 + [pl.BlockSpec(piece.shape, whole) for piece in pieces],
            out_specs=[spec] * (3 if keep else 1),
            scratch_shapes=stores(),
        ),
        out_shape=[jax.ShapeDtypeStruct(SHAPE, jnp.bfloat16)] + wide,
        input_output_aliases={2: 0, 3: 1, 4: 2} if keep else {2: 0},
        compiler_params=pltpu.CompilerParams(vmem_limit_bytes=48 << 20),
        cost_estimate=estimate(1.0 if keep else 0.25),
        name=name,
    )(facts, queries, out, sums, stats, *pieces)
    return made


STEP = [(s, s + 1) for s in range(15)]
MIDDLE = [(s // 4) * 4 + (s - 1) % 4 for s in range(14)]
LEG_ONE = [(s, MIDDLE[s]) for s in range(14)]
LEG_TWO = [(MIDDLE[s], s + 2) for s in range(14)]


def body(queries, keys, values, doc_lengths):
    tokens = queries.shape[0]
    scale = math.log2(math.e) / math.sqrt(queries.shape[2])
    kv = jnp.concatenate([keys.reshape(tokens, 512), values.reshape(tokens, 512)], axis=1)
    cut = tokens - FORWARD
    middle = cut // 32 * 16
    near_high = lax.ppermute(kv[cut:], "ctx", STEP)
    one_low = lax.ppermute(kv[:middle], "ctx", LEG_ONE)
    near_low = lax.ppermute(kv[:cut], "ctx", STEP)
    one_mid = lax.ppermute(kv[middle:cut], "ctx", LEG_ONE)
    far_high = lax.ppermute(near_high, "ctx", STEP)
    far_low = lax.ppermute(one_low, "ctx", LEG_TWO)
    far_mid = lax.ppermute(one_mid, "ctx", LEG_TWO)

    first = lax.axis_index("ctx") * tokens
    lengths = doc_lengths[0]
    order = jnp.arange(lengths.shape[0])
    ends = jnp.sum(jnp.where(order[:, None] <= order[None, :], lengths[:, None], 0), axis=0)
    position = first + jnp.arange(tokens, dtype=jnp.int32)
    starts = jnp.max(jnp.where(ends[None, :] <= position[:, None], ends[None, :], 0), axis=1)
    allowed = (position[None, :] <= position[:, None]) & (position[None, :] >= starts[:, None])
    bias = jnp.where(allowed, 0.0, NEG).astype(jnp.float32).reshape(tokens, 1, tokens)
    start = jnp.max(jnp.where(ends <= first, ends, 0))
    end = jnp.min(jnp.where(ends > first, ends, jnp.iinfo(jnp.int32).max))
    reach = jnp.minimum(end - first, tokens)
    near_facts = jnp.stack(
        [jnp.where(start < first, reach, 0), jnp.maximum(start - first + tokens, 0)]
    ).astype(jnp.int32)
    far_facts = jnp.stack(
        [jnp.where(start < first - tokens, reach, 0), jnp.maximum(start - first + 2 * tokens, 0)]
    ).astype(jnp.int32)

    out, sums, stats = own_tile(queries, bias, kv, scale)
    out, sums, stats = back_tile(
        near_facts, queries, out, sums, stats, [near_low, near_high], scale, True, "near_tile"
    )
    [out] = back_tile(
        far_facts, queries, out, sums, stats, [far_low, far_mid, far_high], scale, False, "far_tile"
    )
    return out


def solution(mesh):
    placed = (
        P(("dp", "ctx"), None, None),
        P(("dp", "ctx"), None, None),
        P(("dp", "ctx"), None, None),
        P("dp", None),
    )
    return jax.shard_map(
        body, mesh=mesh, in_specs=placed, out_specs=P(("dp", "ctx"), None, None), check_vma=False
    )
```

```python
import functools
import math

import jax
import jax.numpy as jnp
from jax import lax
from jax.experimental import pallas as pl
from jax.experimental.pallas import tpu as pltpu
from jax.sharding import PartitionSpec as P

CHUNK = 128
SUB = 32
PAIR = 16
FORWARD = 192
CUT = 320
NEG = -1e30


def attend(query_group, key_part, value_part, bias, scale):
    scores = lax.dot_general(
        query_group, key_part, (((1,), (1,)), ((), ())), preferred_element_type=jnp.float32
    )
    rows, width = scores.shape
    if bias is not None:
        scores = (scores.reshape(rows // 8, 8, width) + bias).reshape(rows, width)
    maxima = jnp.max(scores, axis=-1, keepdims=True)
    weights = jnp.exp2((scores - maxima) * scale).astype(jnp.bfloat16)
    both = jnp.dot(weights, value_part, preferred_element_type=jnp.float32)
    return maxima, both[:, 128:], both[:, :128]


def stage_heads(pieces, key_store, value_store, pair):
    for half in range(2):
        at = 0
        for piece in pieces:
            count = piece.shape[0]
            key_at = pl.multiple_of((pair * 2 + half) * 128, 128)
            value_at = pl.multiple_of(512 + (pair * 2 + half) * 128, 128)
            key_store[half, at : at + count, :] = piece[:, pl.ds(key_at, 128)]
            value_store[half, at : at + count, :128] = piece[:, pl.ds(value_at, 128)]
            value_store[half, at : at + count, 128:] = jnp.ones((count, 128), jnp.bfloat16)
            at += count


def group_rows(ref, rows, half):
    block = ref[rows, :, :].astype(jnp.float32)
    return block[:, half * 8 : half * 8 + 8, :].reshape(-1, 128)


def ungroup(parts):
    return jnp.concatenate([part.reshape(-1, 8, 128) for part in parts], axis=1)


def own_kernel(scale, pair, later, q_ref, bias_ref, kv_ref, *refs):
    out_ref, mean_ref, log_ref = refs[-5 - len(later) : -2 - len(later)]
    later_refs = refs[-2 - len(later) : -2]
    key_store, value_store = refs[-2:]
    chunk = pl.program_id(0)

    @pl.when(chunk == 0)
    def _():
        stage_heads([kv_ref], key_store, value_store, pair)
        for (low, high), later_ref in zip(later, later_refs):
            later_ref[...] = kv_ref[low:high, :]

    def work(width):
        for first in range(0, CHUNK, SUB):
            rows = slice(first, first + SUB)
            means, logs = [], []
            for half in range(2):
                group = group_rows(q_ref, rows, half).astype(jnp.bfloat16)
                maxima, total, output = attend(
                    group,
                    key_store[half, :width, :],
                    value_store[half, :width, :],
                    bias_ref[rows, :, :width],
                    scale,
                )
                means.append(output / total)
                logs.append(maxima * scale + jnp.log2(total))
            mean = ungroup(means)
            out_ref[rows, :, :] = mean.astype(jnp.bfloat16)
            mean_ref[rows, :, :] = mean
            log_ref[rows, :, :] = ungroup(logs)

    pl.when(chunk * CHUNK < 256)(lambda: work(256))
    pl.when(chunk * CHUNK >= 256)(lambda: work(512))


def back_kernel(scale, count, keep, facts, q_ref, old_out, old_mean, old_log, *refs):
    pieces = refs[:count]
    out_ref = refs[count]
    mean_ref, log_ref = refs[count + 1 : count + 3] if keep else (None, None)
    key_store, value_store = refs[-2:]
    pair, chunk = pl.program_id(0), pl.program_id(1)
    row_limit, key_low = facts[0], facts[1]
    live = row_limit - chunk * CHUNK

    @pl.when((chunk == 0) & (row_limit > 0))
    def _():
        stage_heads(pieces, key_store, value_store, pair)

    def work(live_rows, low):
        position = lax.broadcasted_iota(jnp.int32, (1, 1, 512 - low), 2) + low
        bias = jnp.where(position >= key_low, 0.0, NEG).astype(jnp.float32)
        for first in range(0, live_rows, SUB):
            rows = slice(first, first + SUB)
            means, logs = [], []
            for half in range(2):
                group = group_rows(q_ref, rows, half).astype(jnp.bfloat16)
                maxima, total, output = attend(
                    group, key_store[half, low:, :], value_store[half, low:, :], bias, scale
                )
                token = first + lax.broadcasted_iota(jnp.int32, (SUB, 8, 1), 0)
                level = jnp.where((token < live).reshape(-1, 1), maxima * scale, NEG)
                before = group_rows(old_mean, rows, half)
                old_level = group_rows(old_log, rows, half)
                ahead = old_level - level
                small = jnp.exp2(-jnp.abs(ahead))
                old_part = jnp.where(ahead >= 0, 1.0, small)
                new_part = jnp.where(ahead >= 0, small, 1.0)
                whole = old_part + new_part * total
                means.append((old_part * before + new_part * output) / whole)
                if keep:
                    logs.append(jnp.maximum(old_level, level) + jnp.log2(whole))
            mean = ungroup(means)
            out_ref[rows, :, :] = mean.astype(jnp.bfloat16)
            if keep:
                mean_ref[rows, :, :] = mean
                log_ref[rows, :, :] = ungroup(logs)
        if live_rows < CHUNK:
            rows = slice(live_rows, CHUNK)
            out_ref[rows, :, :] = old_mean[rows, :, :].astype(jnp.bfloat16)
            if keep:
                mean_ref[rows, :, :] = old_mean[rows, :, :]
                log_ref[rows, :, :] = old_log[rows, :, :]

    lows = (0, 256) if keep else (0, 256, 384)
    for low, beyond in zip(lows, lows[1:] + (512,)):
        wide = (key_low >= low) & (key_low < beyond)
        pl.when((live > CHUNK // 2) & wide)(functools.partial(work, CHUNK, low))
        pl.when((live > 0) & (live <= CHUNK // 2) & wide)(functools.partial(work, CHUNK // 2, low))

    @pl.when((live <= 0) & (chunk == 0))
    def _():
        out_ref[...] = old_out[...]


SHAPE = (512, 32, 128)
KEPT_SHAPE = (512 + CHUNK, 32, 128)
BLOCK = (CHUNK, PAIR, 128)


def stores():
    return [
        pltpu.VMEM((2, 512, 128), jnp.bfloat16),
        pltpu.VMEM((2, 512, 256), jnp.bfloat16),
    ]


def estimate(part):
    return pl.CostEstimate(
        flops=int(part * 4.3e9), bytes_accessed=int(part * 24e6), transcendentals=int(part * 8.4e6)
    )


def own_tile(queries, bias, kv, scale, pair, made, later):
    spec = pl.BlockSpec(BLOCK, lambda chunk: (chunk, pair, 0))
    whole = lambda chunk: (0, 0)
    sizes = [(high - low, kv.shape[1]) for low, high in later]
    return pl.pallas_call(
        functools.partial(own_kernel, scale, pair, later),
        grid=(512 // CHUNK,),
        in_specs=[
            spec,
            pl.BlockSpec((CHUNK, 1, 512), lambda chunk: (chunk, 0, 0)),
            pl.BlockSpec(kv.shape, whole),
        ]
        + [pl.BlockSpec(memory_space=pl.ANY)] * len(made),
        out_specs=[spec] * 3 + [pl.BlockSpec(size, whole) for size in sizes],
        out_shape=[jax.ShapeDtypeStruct(SHAPE, jnp.bfloat16)]
        + [jax.ShapeDtypeStruct(SHAPE, jnp.float32)] * 2
        + [jax.ShapeDtypeStruct(size, jnp.bfloat16) for size in sizes],
        input_output_aliases={3 + place: place for place in range(len(made))},
        scratch_shapes=stores(),
        compiler_params=pltpu.CompilerParams(vmem_limit_bytes=58 << 20),
        cost_estimate=estimate(0.5),
        name="own_tile",
    )(queries, bias, kv, *made)


def back_tile(facts, queries, out, means, logs, pieces, scale, keep, name):
    def at(pair, chunk, facts):
        last = jnp.maximum((facts[0] + CHUNK - 1) // CHUNK - 1, 0)
        return (jnp.minimum(chunk, last), pair, 0)

    def kept(pair, chunk, facts):
        row, column, lane = at(pair, chunk, facts)
        some = facts[2] > 0
        return (jnp.where(some, row, 512 // CHUNK), jnp.where(some, column, 0), lane)

    spec, kept_spec = pl.BlockSpec(BLOCK, at), pl.BlockSpec(BLOCK, kept)
    first_spec = pl.BlockSpec(BLOCK, lambda pair, chunk, facts: (0, pair, 0))
    return pl.pallas_call(
        functools.partial(back_kernel, scale, len(pieces), keep),
        grid_spec=pltpu.PrefetchScalarGridSpec(
            num_scalar_prefetch=1,
            grid=(2, 512 // CHUNK),
            in_specs=[spec, first_spec, spec, spec]
            + [pl.BlockSpec(piece.shape, lambda pair, chunk, facts: (0, 0)) for piece in pieces],
            out_specs=[spec, kept_spec, kept_spec] if keep else [spec],
            scratch_shapes=stores(),
        ),
        out_shape=[jax.ShapeDtypeStruct(SHAPE, jnp.bfloat16)]
        + [jax.ShapeDtypeStruct(KEPT_SHAPE, jnp.float32)] * (2 if keep else 0),
        input_output_aliases={2: 0},
        compiler_params=pltpu.CompilerParams(vmem_limit_bytes=58 << 20),
        cost_estimate=estimate(1.0 if keep else 0.25),
        name=name,
    )(facts, queries, out, means, logs, *pieces)


STEP = [(s, s + 1) for s in range(15)]
MIDDLE = [(s // 4) * 4 + (s - 1) % 4 for s in range(14)]
LEG_ONE = [(s, MIDDLE[s]) for s in range(14)]
LEG_TWO = [(MIDDLE[s], s + 2) for s in range(14)]


def body(queries, keys, values, doc_lengths):
    tokens = queries.shape[0]
    scale = math.log2(math.e) / math.sqrt(queries.shape[2])
    kv = jnp.concatenate([keys.reshape(tokens, 512), values.reshape(tokens, 512)], axis=1)
    middle = (tokens + FORWARD) // 32 * 16
    near_low = lax.ppermute(kv[:CUT], "ctx", STEP)
    one_mid = lax.ppermute(kv[FORWARD:middle], "ctx", LEG_ONE)

    first = lax.axis_index("ctx") * tokens
    lengths = doc_lengths[0]
    order = jnp.arange(lengths.shape[0])
    ends = jnp.sum(jnp.where(order[:, None] <= order[None, :], lengths[:, None], 0), axis=0)
    position = first + jnp.arange(tokens, dtype=jnp.int32)
    starts = jnp.max(jnp.where(ends[None, :] <= position[:, None], ends[None, :], 0), axis=1)
    allowed = (position[None, :] <= position[:, None]) & (position[None, :] >= starts[:, None])
    bias = jnp.where(allowed, 0.0, NEG).astype(jnp.float32).reshape(tokens, 1, tokens)
    start = jnp.max(jnp.where(ends <= first, ends, 0))
    end = jnp.min(jnp.where(ends > first, ends, jnp.iinfo(jnp.int32).max))
    reach = jnp.minimum(end - first, tokens)
    near_rows = jnp.where(start < first, reach, 0)
    far_rows = jnp.where(start < first - tokens, reach, 0)
    near_facts = jnp.stack([near_rows, jnp.maximum(start - first + tokens, 0), far_rows])
    far_facts = jnp.stack([far_rows, jnp.maximum(start - first + 2 * tokens, 0), far_rows])

    *made, later_near, later_one = own_tile(
        queries, bias, kv, scale, 0, [], [(CUT, tokens), (middle, tokens)]
    )
    near_high = lax.ppermute(later_near, "ctx", STEP)
    one_high = lax.ppermute(later_one, "ctx", LEG_ONE)
    out, means, logs = own_tile(queries, bias, kv, scale, 1, made, [])
    far_low = lax.ppermute(near_low[:FORWARD], "ctx", STEP)
    far_mid = lax.ppermute(one_mid, "ctx", LEG_TWO)
    far_high = lax.ppermute(one_high, "ctx", LEG_TWO)
    out, means, logs = back_tile(
        near_facts, queries, out, means, logs, [near_low, near_high], scale, True, "near_tile"
    )
    [out] = back_tile(
        far_facts, queries, out, means, logs, [far_low, far_mid, far_high], scale, False, "far_tile"
    )
    return out


def solution(mesh):
    placed = (
        P(("dp", "ctx"), None, None),
        P(("dp", "ctx"), None, None),
        P(("dp", "ctx"), None, None),
        P("dp", None),
    )
    return jax.shard_map(
        body, mesh=mesh, in_specs=placed, out_specs=P(("dp", "ctx"), None, None), check_vma=False
    )
```

```python
import functools
import math

import jax
import jax.numpy as jnp
from jax import lax
from jax.experimental import pallas as pl
from jax.experimental.pallas import tpu as pltpu
from jax.sharding import PartitionSpec as P

CHUNK = 128
SUB = 32
PAIR = 16
FORWARD = 192
CUT = 320
NEG = -1e30


def attend(query_group, key_part, value_part, bias, scale):
    scores = lax.dot_general(
        query_group, key_part, (((1,), (1,)), ((), ())), preferred_element_type=jnp.float32
    )
    rows, width = scores.shape
    if bias is not None:
        scores = (scores.reshape(rows // 8, 8, width) + bias).reshape(rows, width)
    maxima = jnp.max(scores, axis=-1, keepdims=True)
    weights = jnp.exp2((scores - maxima) * scale).astype(jnp.bfloat16)
    both = jnp.dot(weights, value_part, preferred_element_type=jnp.float32)
    return maxima, both[:, 128:], both[:, :128]


def stage_heads(pieces, key_store, value_store, pair):
    for half in range(2):
        at = 0
        for piece in pieces:
            count = piece.shape[0]
            key_at = pl.multiple_of((pair * 2 + half) * 128, 128)
            value_at = pl.multiple_of(512 + (pair * 2 + half) * 128, 128)
            key_store[half, at : at + count, :] = piece[:, pl.ds(key_at, 128)]
            value_store[half, at : at + count, :128] = piece[:, pl.ds(value_at, 128)]
            value_store[half, at : at + count, 128:] = jnp.ones((count, 128), jnp.bfloat16)
            at += count


def group_rows(ref, rows, half):
    block = ref[rows, :, :].astype(jnp.float32)
    return block[:, half * 8 : half * 8 + 8, :].reshape(-1, 128)


def ungroup(parts):
    return jnp.concatenate([part.reshape(-1, 8, 128) for part in parts], axis=1)


def own_kernel(scale, q_ref, bias_ref, kv_ref, out_ref, mean_ref, log_ref, key_store, value_store):
    pair, chunk = pl.program_id(0), pl.program_id(1)

    @pl.when(chunk == 0)
    def _():
        stage_heads([kv_ref], key_store, value_store, pair)

    def work(width):
        for first in range(0, CHUNK, SUB):
            rows = slice(first, first + SUB)
            means, logs = [], []
            for half in range(2):
                group = group_rows(q_ref, rows, half).astype(jnp.bfloat16)
                maxima, total, output = attend(
                    group,
                    key_store[half, :width, :],
                    value_store[half, :width, :],
                    bias_ref[rows, :, :width],
                    scale,
                )
                means.append(output / total)
                logs.append(maxima * scale + jnp.log2(total))
            mean = ungroup(means)
            out_ref[rows, :, :] = mean.astype(jnp.bfloat16)
            mean_ref[rows, :, :] = mean
            log_ref[rows, :, :] = ungroup(logs)

    pl.when(chunk * CHUNK < 256)(lambda: work(256))
    pl.when(chunk * CHUNK >= 256)(lambda: work(512))


def back_kernel(scale, count, keep, facts, q_ref, old_out, old_mean, old_log, *refs):
    pieces = refs[:count]
    out_ref = refs[count]
    mean_ref, log_ref = refs[count + 1 : count + 3] if keep else (None, None)
    key_store, value_store = refs[-2:]
    pair, chunk = pl.program_id(0), pl.program_id(1)
    row_limit, key_low = facts[0], facts[1]
    live = row_limit - chunk * CHUNK

    @pl.when((chunk == 0) & (row_limit > 0))
    def _():
        stage_heads(pieces, key_store, value_store, pair)

    def work(live_rows, low):
        position = lax.broadcasted_iota(jnp.int32, (1, 1, 512 - low), 2) + low
        bias = jnp.where(position >= key_low, 0.0, NEG).astype(jnp.float32)
        for first in range(0, live_rows, SUB):
            rows = slice(first, first + SUB)
            means, logs = [], []
            for half in range(2):
                group = group_rows(q_ref, rows, half).astype(jnp.bfloat16)
                maxima, total, output = attend(
                    group, key_store[half, low:, :], value_store[half, low:, :], bias, scale
                )
                token = first + lax.broadcasted_iota(jnp.int32, (SUB, 8, 1), 0)
                level = jnp.where((token < live).reshape(-1, 1), maxima * scale, NEG)
                before = group_rows(old_mean, rows, half)
                old_level = group_rows(old_log, rows, half)
                ahead = old_level - level
                small = jnp.exp2(-jnp.abs(ahead))
                old_part = jnp.where(ahead >= 0, 1.0, small)
                new_part = jnp.where(ahead >= 0, small, 1.0)
                whole = old_part + new_part * total
                means.append((old_part * before + new_part * output) / whole)
                if keep:
                    logs.append(jnp.maximum(old_level, level) + jnp.log2(whole))
            mean = ungroup(means)
            out_ref[rows, :, :] = mean.astype(jnp.bfloat16)
            if keep:
                mean_ref[rows, :, :] = mean
                log_ref[rows, :, :] = ungroup(logs)
        if live_rows < CHUNK:
            rows = slice(live_rows, CHUNK)
            out_ref[rows, :, :] = old_mean[rows, :, :].astype(jnp.bfloat16)
            if keep:
                mean_ref[rows, :, :] = old_mean[rows, :, :]
                log_ref[rows, :, :] = old_log[rows, :, :]

    lows = (0, 256) if keep else (0, 256, 384)
    for low, beyond in zip(lows, lows[1:] + (512,)):
        wide = (key_low >= low) & (key_low < beyond)
        pl.when((live > CHUNK // 2) & wide)(functools.partial(work, CHUNK, low))
        pl.when((live > 0) & (live <= CHUNK // 2) & wide)(functools.partial(work, CHUNK // 2, low))

    @pl.when((live <= 0) & (chunk == 0))
    def _():
        out_ref[...] = old_out[...]


SHAPE = (512, 32, 128)
KEPT_SHAPE = (512 + CHUNK, 32, 128)
BLOCK = (CHUNK, PAIR, 128)


def stores():
    return [
        pltpu.VMEM((2, 512, 128), jnp.bfloat16),
        pltpu.VMEM((2, 512, 256), jnp.bfloat16),
    ]


def estimate(part):
    return pl.CostEstimate(
        flops=int(part * 4.3e9), bytes_accessed=int(part * 24e6), transcendentals=int(part * 8.4e6)
    )


def own_tile(queries, bias, kv, scale):
    spec = pl.BlockSpec(BLOCK, lambda pair, chunk: (chunk, pair, 0))
    return pl.pallas_call(
        functools.partial(own_kernel, scale),
        grid=(2, 512 // CHUNK),
        in_specs=[
            spec,
            pl.BlockSpec((CHUNK, 1, 512), lambda pair, chunk: (chunk, 0, 0)),
            pl.BlockSpec(kv.shape, lambda pair, chunk: (0, 0)),
        ],
        out_specs=[spec] * 3,
        out_shape=[jax.ShapeDtypeStruct(SHAPE, jnp.bfloat16)]
        + [jax.ShapeDtypeStruct(SHAPE, jnp.float32)] * 2,
        scratch_shapes=stores(),
        compiler_params=pltpu.CompilerParams(vmem_limit_bytes=58 << 20),
        cost_estimate=estimate(1.0),
        name="own_tile",
    )(queries, bias, kv)


def back_tile(facts, queries, out, means, logs, pieces, scale, keep, name):
    def at(pair, chunk, facts):
        last = jnp.maximum((facts[0] + CHUNK - 1) // CHUNK - 1, 0)
        return (jnp.minimum(chunk, last), pair, 0)

    def kept(pair, chunk, facts):
        row, column, lane = at(pair, chunk, facts)
        some = facts[2] > 0
        return (jnp.where(some, row, 512 // CHUNK), jnp.where(some, column, 0), lane)

    spec, kept_spec = pl.BlockSpec(BLOCK, at), pl.BlockSpec(BLOCK, kept)
    first_spec = pl.BlockSpec(BLOCK, lambda pair, chunk, facts: (0, pair, 0))
    return pl.pallas_call(
        functools.partial(back_kernel, scale, len(pieces), keep),
        grid_spec=pltpu.PrefetchScalarGridSpec(
            num_scalar_prefetch=1,
            grid=(2, 512 // CHUNK),
            in_specs=[spec, first_spec, spec, spec]
            + [pl.BlockSpec(piece.shape, lambda pair, chunk, facts: (0, 0)) for piece in pieces],
            out_specs=[spec, kept_spec, kept_spec] if keep else [spec],
            scratch_shapes=stores(),
        ),
        out_shape=[jax.ShapeDtypeStruct(SHAPE, jnp.bfloat16)]
        + [jax.ShapeDtypeStruct(KEPT_SHAPE, jnp.float32)] * (2 if keep else 0),
        input_output_aliases={2: 0},
        compiler_params=pltpu.CompilerParams(vmem_limit_bytes=58 << 20),
        cost_estimate=estimate(1.0 if keep else 0.25),
        name=name,
    )(facts, queries, out, means, logs, *pieces)


STEP = [(s, s + 1) for s in range(15)]
MIDDLE = [(s // 4) * 4 + (s - 1) % 4 for s in range(14)]
LEG_ONE = [(s, MIDDLE[s]) for s in range(14)]
LEG_TWO = [(MIDDLE[s], s + 2) for s in range(14)]


def body(queries, keys, values, doc_lengths):
    tokens = queries.shape[0]
    scale = math.log2(math.e) / math.sqrt(queries.shape[2])
    kv = jnp.concatenate([keys.reshape(tokens, 512), values.reshape(tokens, 512)], axis=1)
    middle = (tokens + FORWARD) // 32 * 16
    near_low = lax.ppermute(kv[:CUT], "ctx", STEP)
    one_mid = lax.ppermute(kv[FORWARD:middle], "ctx", LEG_ONE)
    near_high = lax.ppermute(kv[CUT:], "ctx", STEP)
    one_high = lax.ppermute(kv[middle:], "ctx", LEG_ONE)

    first = lax.axis_index("ctx") * tokens
    lengths = doc_lengths[0]
    order = jnp.arange(lengths.shape[0])
    ends = jnp.sum(jnp.where(order[:, None] <= order[None, :], lengths[:, None], 0), axis=0)
    position = first + jnp.arange(tokens, dtype=jnp.int32)
    starts = jnp.max(jnp.where(ends[None, :] <= position[:, None], ends[None, :], 0), axis=1)
    allowed = (position[None, :] <= position[:, None]) & (position[None, :] >= starts[:, None])
    bias = jnp.where(allowed, 0.0, NEG).astype(jnp.float32).reshape(tokens, 1, tokens)
    start = jnp.max(jnp.where(ends <= first, ends, 0))
    end = jnp.min(jnp.where(ends > first, ends, jnp.iinfo(jnp.int32).max))
    reach = jnp.minimum(end - first, tokens)
    near_rows = jnp.where(start < first, reach, 0)
    far_rows = jnp.where(start < first - tokens, reach, 0)
    near_facts = jnp.stack([near_rows, jnp.maximum(start - first + tokens, 0), far_rows])
    far_facts = jnp.stack([far_rows, jnp.maximum(start - first + 2 * tokens, 0), far_rows])

    out, means, logs = own_tile(queries, bias, kv, scale)
    far_low = lax.ppermute(near_low[:FORWARD], "ctx", STEP)
    far_mid = lax.ppermute(one_mid, "ctx", LEG_TWO)
    far_high = lax.ppermute(one_high, "ctx", LEG_TWO)
    out, means, logs = back_tile(
        near_facts, queries, out, means, logs, [near_low, near_high], scale, True, "near_tile"
    )
    [out] = back_tile(
        far_facts, queries, out, means, logs, [far_low, far_mid, far_high], scale, False, "far_tile"
    )
    return out


def solution(mesh):
    placed = (
        P(("dp", "ctx"), None, None),
        P(("dp", "ctx"), None, None),
        P(("dp", "ctx"), None, None),
        P("dp", None),
    )
    return jax.shard_map(
        body, mesh=mesh, in_specs=placed, out_specs=P(("dp", "ctx"), None, None), check_vma=False
    )
```

```python
import functools
import math

import jax
import jax.numpy as jnp
from jax import lax
from jax.experimental import pallas as pl
from jax.experimental.pallas import tpu as pltpu
from jax.sharding import PartitionSpec as P

CHUNK = 256
SUB = 32
PAIR = 16
FORWARD = 192
CUT = 320
NEG = -1e30


def attend(query_group, key_part, value_part, bias, scale):
    scores = lax.dot_general(
        query_group, key_part, (((1,), (1,)), ((), ())), preferred_element_type=jnp.float32
    )
    rows, width = scores.shape
    if bias is not None:
        scores = (scores.reshape(rows // 8, 8, width) + bias).reshape(rows, width)
    maxima = jnp.max(scores, axis=-1, keepdims=True)
    weights = jnp.exp2((scores - maxima) * scale).astype(jnp.bfloat16)
    both = jnp.dot(weights, value_part, preferred_element_type=jnp.float32)
    return maxima, both[:, 128:], both[:, :128]


def stage_heads(pieces, key_store, value_store, pair):
    for half in range(2):
        at = 0
        for piece in pieces:
            count = piece.shape[0]
            key_at = pl.multiple_of((pair * 2 + half) * 128, 128)
            value_at = pl.multiple_of(512 + (pair * 2 + half) * 128, 128)
            key_store[half, at : at + count, :] = piece[:, pl.ds(key_at, 128)]
            value_store[half, at : at + count, :128] = piece[:, pl.ds(value_at, 128)]
            value_store[half, at : at + count, 128:] = jnp.ones((count, 128), jnp.bfloat16)
            at += count


def group_rows(ref, rows, half):
    block = ref[rows, :, :].astype(jnp.float32)
    return block[:, half * 8 : half * 8 + 8, :].reshape(-1, 128)


def ungroup(parts):
    return jnp.concatenate([part.reshape(-1, 8, 128) for part in parts], axis=1)


def own_kernel(scale, q_ref, bias_ref, kv_ref, out_ref, mean_ref, log_ref, key_store, value_store):
    pair, chunk = pl.program_id(0), pl.program_id(1)

    @pl.when(chunk == 0)
    def _():
        stage_heads([kv_ref], key_store, value_store, pair)

    def work(width):
        for first in range(0, CHUNK, SUB):
            rows = slice(first, first + SUB)
            means, logs = [], []
            for half in range(2):
                group = group_rows(q_ref, rows, half).astype(jnp.bfloat16)
                maxima, total, output = attend(
                    group,
                    key_store[half, :width, :],
                    value_store[half, :width, :],
                    bias_ref[rows, :, :width],
                    scale,
                )
                means.append(output / total)
                logs.append(maxima * scale + jnp.log2(total))
            mean = ungroup(means)
            out_ref[rows, :, :] = mean.astype(jnp.bfloat16)
            mean_ref[rows, :, :] = mean
            log_ref[rows, :, :] = ungroup(logs)

    pl.when(chunk * CHUNK < 256)(lambda: work(256))
    pl.when(chunk * CHUNK >= 256)(lambda: work(512))


def back_kernel(scale, count, keep, facts, q_ref, old_out, old_mean, old_log, *refs):
    pieces = refs[:count]
    out_ref = refs[count]
    mean_ref, log_ref = refs[count + 1 : count + 3] if keep else (None, None)
    key_store, value_store = refs[-2:]
    pair, chunk = pl.program_id(0), pl.program_id(1)
    row_limit, key_low = facts[0], facts[1]
    live = row_limit - chunk * CHUNK

    @pl.when((chunk == 0) & (row_limit > 0))
    def _():
        stage_heads(pieces, key_store, value_store, pair)

    def work(live_rows, low):
        position = lax.broadcasted_iota(jnp.int32, (1, 1, 512 - low), 2) + low
        bias = jnp.where(position >= key_low, 0.0, NEG).astype(jnp.float32)
        for first in range(0, live_rows, SUB):
            rows = slice(first, first + SUB)
            means, logs = [], []
            for half in range(2):
                group = group_rows(q_ref, rows, half).astype(jnp.bfloat16)
                maxima, total, output = attend(
                    group, key_store[half, low:, :], value_store[half, low:, :], bias, scale
                )
                token = first + lax.broadcasted_iota(jnp.int32, (SUB, 8, 1), 0)
                level = jnp.where((token < live).reshape(-1, 1), maxima * scale, NEG)
                before = group_rows(old_mean, rows, half)
                old_level = group_rows(old_log, rows, half)
                ahead = old_level - level
                small = jnp.exp2(-jnp.abs(ahead))
                old_part = jnp.where(ahead >= 0, 1.0, small)
                new_part = jnp.where(ahead >= 0, small, 1.0)
                whole = old_part + new_part * total
                means.append((old_part * before + new_part * output) / whole)
                if keep:
                    logs.append(jnp.maximum(old_level, level) + jnp.log2(whole))
            mean = ungroup(means)
            out_ref[rows, :, :] = mean.astype(jnp.bfloat16)
            if keep:
                mean_ref[rows, :, :] = mean
                log_ref[rows, :, :] = ungroup(logs)
        if live_rows < CHUNK:
            rows = slice(live_rows, CHUNK)
            out_ref[rows, :, :] = old_mean[rows, :, :].astype(jnp.bfloat16)
            if keep:
                mean_ref[rows, :, :] = old_mean[rows, :, :]
                log_ref[rows, :, :] = old_log[rows, :, :]

    lows = (0, 256) if keep else (0, 256, 384)
    for low, beyond in zip(lows, lows[1:] + (512,)):
        wide = (key_low >= low) & (key_low < beyond)
        pl.when((live > CHUNK // 2) & wide)(functools.partial(work, CHUNK, low))
        pl.when((live > 0) & (live <= CHUNK // 2) & wide)(functools.partial(work, CHUNK // 2, low))

    @pl.when((live <= 0) & (chunk == 0))
    def _():
        out_ref[...] = old_out[...]


SHAPE = (512, 32, 128)
KEPT_SHAPE = (512 + CHUNK, 32, 128)
BLOCK = (CHUNK, PAIR, 128)


def stores():
    return [
        pltpu.VMEM((2, 512, 128), jnp.bfloat16),
        pltpu.VMEM((2, 512, 256), jnp.bfloat16),
    ]


def estimate(part):
    return pl.CostEstimate(
        flops=int(part * 4.3e9), bytes_accessed=int(part * 24e6), transcendentals=int(part * 8.4e6)
    )


def own_tile(queries, bias, kv, scale):
    spec = pl.BlockSpec(BLOCK, lambda pair, chunk: (chunk, pair, 0))
    return pl.pallas_call(
        functools.partial(own_kernel, scale),
        grid=(2, 512 // CHUNK),
        in_specs=[
            spec,
            pl.BlockSpec((CHUNK, 1, 512), lambda pair, chunk: (chunk, 0, 0)),
            pl.BlockSpec(kv.shape, lambda pair, chunk: (0, 0)),
        ],
        out_specs=[spec] * 3,
        out_shape=[jax.ShapeDtypeStruct(SHAPE, jnp.bfloat16)]
        + [jax.ShapeDtypeStruct(SHAPE, jnp.float32)] * 2,
        scratch_shapes=stores(),
        compiler_params=pltpu.CompilerParams(vmem_limit_bytes=58 << 20),
        cost_estimate=estimate(1.0),
        name="own_tile",
    )(queries, bias, kv)


def back_tile(facts, queries, out, means, logs, pieces, scale, keep, name):
    def at(pair, chunk, facts):
        last = jnp.maximum((facts[0] + CHUNK - 1) // CHUNK - 1, 0)
        return (jnp.minimum(chunk, last), pair, 0)

    def kept(pair, chunk, facts):
        row, column, lane = at(pair, chunk, facts)
        some = facts[2] > 0
        return (jnp.where(some, row, 512 // CHUNK), jnp.where(some, column, 0), lane)

    spec, kept_spec = pl.BlockSpec(BLOCK, at), pl.BlockSpec(BLOCK, kept)
    first_spec = pl.BlockSpec(BLOCK, lambda pair, chunk, facts: (0, pair, 0))
    return pl.pallas_call(
        functools.partial(back_kernel, scale, len(pieces), keep),
        grid_spec=pltpu.PrefetchScalarGridSpec(
            num_scalar_prefetch=1,
            grid=(2, 512 // CHUNK),
            in_specs=[spec, first_spec, spec, spec]
            + [pl.BlockSpec(piece.shape, lambda pair, chunk, facts: (0, 0)) for piece in pieces],
            out_specs=[spec, kept_spec, kept_spec] if keep else [spec],
            scratch_shapes=stores(),
        ),
        out_shape=[jax.ShapeDtypeStruct(SHAPE, jnp.bfloat16)]
        + [jax.ShapeDtypeStruct(KEPT_SHAPE, jnp.float32)] * (2 if keep else 0),
        input_output_aliases={2: 0},
        compiler_params=pltpu.CompilerParams(vmem_limit_bytes=58 << 20),
        cost_estimate=estimate(1.0 if keep else 0.25),
        name=name,
    )(facts, queries, out, means, logs, *pieces)


STEP = [(s, s + 1) for s in range(15)]
MIDDLE = [(s // 4) * 4 + (s - 1) % 4 for s in range(14)]
LEG_ONE = [(s, MIDDLE[s]) for s in range(14)]
LEG_TWO = [(MIDDLE[s], s + 2) for s in range(14)]


def body(queries, keys, values, doc_lengths):
    tokens = queries.shape[0]
    scale = math.log2(math.e) / math.sqrt(queries.shape[2])
    kv = jnp.concatenate([keys.reshape(tokens, 512), values.reshape(tokens, 512)], axis=1)
    middle = (tokens + FORWARD) // 32 * 16
    near_low = lax.ppermute(kv[:CUT], "ctx", STEP)
    one_mid = lax.ppermute(kv[FORWARD:middle], "ctx", LEG_ONE)
    near_high = lax.ppermute(kv[CUT:], "ctx", STEP)
    one_high = lax.ppermute(kv[middle:], "ctx", LEG_ONE)

    first = lax.axis_index("ctx") * tokens
    lengths = doc_lengths[0]
    order = jnp.arange(lengths.shape[0])
    ends = jnp.sum(jnp.where(order[:, None] <= order[None, :], lengths[:, None], 0), axis=0)
    position = first + jnp.arange(tokens, dtype=jnp.int32)
    starts = jnp.max(jnp.where(ends[None, :] <= position[:, None], ends[None, :], 0), axis=1)
    allowed = (position[None, :] <= position[:, None]) & (position[None, :] >= starts[:, None])
    bias = jnp.where(allowed, 0.0, NEG).astype(jnp.float32).reshape(tokens, 1, tokens)
    start = jnp.max(jnp.where(ends <= first, ends, 0))
    end = jnp.min(jnp.where(ends > first, ends, jnp.iinfo(jnp.int32).max))
    reach = jnp.minimum(end - first, tokens)
    near_rows = jnp.where(start < first, reach, 0)
    far_rows = jnp.where(start < first - tokens, reach, 0)
    near_facts = jnp.stack([near_rows, jnp.maximum(start - first + tokens, 0), far_rows])
    far_facts = jnp.stack([far_rows, jnp.maximum(start - first + 2 * tokens, 0), far_rows])

    out, means, logs = own_tile(queries, bias, kv, scale)
    far_low = lax.ppermute(near_low[:FORWARD], "ctx", STEP)
    far_mid = lax.ppermute(one_mid, "ctx", LEG_TWO)
    far_high = lax.ppermute(one_high, "ctx", LEG_TWO)
    out, means, logs = back_tile(
        near_facts, queries, out, means, logs, [near_low, near_high], scale, True, "near_tile"
    )
    [out] = back_tile(
        far_facts, queries, out, means, logs, [far_low, far_mid, far_high], scale, False, "far_tile"
    )
    return out


def solution(mesh):
    placed = (
        P(("dp", "ctx"), None, None),
        P(("dp", "ctx"), None, None),
        P(("dp", "ctx"), None, None),
        P("dp", None),
    )
    return jax.shard_map(
        body, mesh=mesh, in_specs=placed, out_specs=P(("dp", "ctx"), None, None), check_vma=False
    )
```

```python
import functools
import math

import jax
import jax.numpy as jnp
from jax import lax
from jax.experimental import pallas as pl
from jax.experimental.pallas import tpu as pltpu
from jax.sharding import PartitionSpec as P

CHUNK = 256
SUB = 32
PAIR = 16
FORWARD = 192
CUT = 320
NEG = -1e30


def attend(query_group, key_part, value_part, bias, scale):
    scores = lax.dot_general(
        query_group, key_part, (((1,), (1,)), ((), ())), preferred_element_type=jnp.float32
    )
    rows, width = scores.shape
    if bias is not None:
        masked = bias.shape[-1]
        head = (scores[:, :masked].reshape(rows // 8, 8, masked) + bias).reshape(rows, masked)
        scores = jnp.concatenate([head, scores[:, masked:]], axis=1) if masked < width else head
    maxima = jnp.max(scores, axis=-1, keepdims=True)
    weights = jnp.exp2((scores - maxima) * scale).astype(jnp.bfloat16)
    both = jnp.dot(weights, value_part, preferred_element_type=jnp.float32)
    return maxima, both[:, 128:], both[:, :128]


def stage_heads(pieces, key_store, value_store, pair):
    for half in range(2):
        at = 0
        for piece in pieces:
            count = piece.shape[0]
            key_at = pl.multiple_of((pair * 2 + half) * 128, 128)
            value_at = pl.multiple_of(512 + (pair * 2 + half) * 128, 128)
            key_store[half, at : at + count, :] = piece[:, pl.ds(key_at, 128)]
            value_store[half, at : at + count, :128] = piece[:, pl.ds(value_at, 128)]
            value_store[half, at : at + count, 128:] = jnp.ones((count, 128), jnp.bfloat16)
            at += count


def group_rows(ref, rows, half):
    block = ref[rows, :, :].astype(jnp.float32)
    return block[:, half * 8 : half * 8 + 8, :].reshape(-1, 128)


def ungroup(parts):
    return jnp.concatenate([part.reshape(-1, 8, 128) for part in parts], axis=1)


def own_kernel(scale, q_ref, bias_ref, kv_ref, out_ref, mean_ref, log_ref, key_store, value_store):
    pair, chunk = pl.program_id(0), pl.program_id(1)

    @pl.when(chunk == 0)
    def _():
        stage_heads([kv_ref], key_store, value_store, pair)

    def work(width):
        for first in range(0, CHUNK, SUB):
            rows = slice(first, first + SUB)
            means, logs = [], []
            for half in range(2):
                group = group_rows(q_ref, rows, half).astype(jnp.bfloat16)
                maxima, total, output = attend(
                    group,
                    key_store[half, :width, :],
                    value_store[half, :width, :],
                    bias_ref[rows, :, :width],
                    scale,
                )
                means.append(output / total)
                logs.append(maxima * scale + jnp.log2(total))
            mean = ungroup(means)
            out_ref[rows, :, :] = mean.astype(jnp.bfloat16)
            mean_ref[rows, :, :] = mean
            log_ref[rows, :, :] = ungroup(logs)

    pl.when(chunk * CHUNK < 256)(lambda: work(256))
    pl.when(chunk * CHUNK >= 256)(lambda: work(512))


def back_kernel(scale, count, keep, facts, q_ref, old_out, old_mean, old_log, *refs):
    pieces = refs[:count]
    out_ref = refs[count]
    mean_ref, log_ref = refs[count + 1 : count + 3] if keep else (None, None)
    key_store, value_store = refs[-2:]
    pair, chunk = pl.program_id(0), pl.program_id(1)
    row_limit, key_low = facts[0], facts[1]
    live = row_limit - chunk * CHUNK

    @pl.when((chunk == 0) & (row_limit > 0))
    def _():
        stage_heads(pieces, key_store, value_store, pair)

    def work(live_rows, low, beyond):
        position = lax.broadcasted_iota(jnp.int32, (1, 1, beyond - low), 2) + low
        bias = jnp.where(position >= key_low, 0.0, NEG).astype(jnp.float32)
        for first in range(0, live_rows, SUB):
            rows = slice(first, first + SUB)
            means, logs = [], []
            for half in range(2):
                group = group_rows(q_ref, rows, half).astype(jnp.bfloat16)
                maxima, total, output = attend(
                    group, key_store[half, low:, :], value_store[half, low:, :], bias, scale
                )
                token = first + lax.broadcasted_iota(jnp.int32, (SUB, 8, 1), 0)
                level = jnp.where((token < live).reshape(-1, 1), maxima * scale, NEG)
                before = group_rows(old_mean, rows, half)
                old_level = group_rows(old_log, rows, half)
                ahead = old_level - level
                small = jnp.exp2(-jnp.abs(ahead))
                old_part = jnp.where(ahead >= 0, 1.0, small)
                new_part = jnp.where(ahead >= 0, small, 1.0)
                whole = old_part + new_part * total
                means.append((old_part * before + new_part * output) / whole)
                if keep:
                    logs.append(jnp.maximum(old_level, level) + jnp.log2(whole))
            mean = ungroup(means)
            out_ref[rows, :, :] = mean.astype(jnp.bfloat16)
            if keep:
                mean_ref[rows, :, :] = mean
                log_ref[rows, :, :] = ungroup(logs)
        if live_rows < CHUNK:
            rows = slice(live_rows, CHUNK)
            out_ref[rows, :, :] = old_mean[rows, :, :].astype(jnp.bfloat16)
            if keep:
                mean_ref[rows, :, :] = old_mean[rows, :, :]
                log_ref[rows, :, :] = old_log[rows, :, :]

    lows = (0, 256) if keep else (0, 256, 384)
    for low, beyond in zip(lows, lows[1:] + (512,)):
        wide = (key_low >= low) & (key_low < beyond)
        pl.when((live > CHUNK // 2) & wide)(functools.partial(work, CHUNK, low, beyond))
        pl.when((live > 0) & (live <= CHUNK // 2) & wide)(functools.partial(work, CHUNK // 2, low, beyond))

    @pl.when((live <= 0) & (chunk == 0))
    def _():
        out_ref[...] = old_out[...]


SHAPE = (512, 32, 128)
KEPT_SHAPE = (512 + CHUNK, 32, 128)
BLOCK = (CHUNK, PAIR, 128)


def stores():
    return [
        pltpu.VMEM((2, 512, 128), jnp.bfloat16),
        pltpu.VMEM((2, 512, 256), jnp.bfloat16),
    ]


def estimate(part):
    return pl.CostEstimate(
        flops=int(part * 4.3e9), bytes_accessed=int(part * 24e6), transcendentals=int(part * 8.4e6)
    )


def own_tile(queries, bias, kv, scale):
    spec = pl.BlockSpec(BLOCK, lambda pair, chunk: (chunk, pair, 0))
    return pl.pallas_call(
        functools.partial(own_kernel, scale),
        grid=(2, 512 // CHUNK),
        in_specs=[
            spec,
            pl.BlockSpec((CHUNK, 1, 512), lambda pair, chunk: (chunk, 0, 0)),
            pl.BlockSpec(kv.shape, lambda pair, chunk: (0, 0)),
        ],
        out_specs=[spec] * 3,
        out_shape=[jax.ShapeDtypeStruct(SHAPE, jnp.bfloat16)]
        + [jax.ShapeDtypeStruct(SHAPE, jnp.float32)] * 2,
        scratch_shapes=stores(),
        compiler_params=pltpu.CompilerParams(vmem_limit_bytes=52 << 20),
        cost_estimate=estimate(1.0),
        name="own_tile",
    )(queries, bias, kv)


def back_tile(facts, queries, out, means, logs, pieces, scale, keep, name):
    def at(pair, chunk, facts):
        last = jnp.maximum((facts[0] + CHUNK - 1) // CHUNK - 1, 0)
        return (jnp.minimum(chunk, last), pair, 0)

    def kept(pair, chunk, facts):
        row, column, lane = at(pair, chunk, facts)
        some = facts[2] > 0
        return (jnp.where(some, row, 512 // CHUNK), jnp.where(some, column, 0), lane)

    spec, kept_spec = pl.BlockSpec(BLOCK, at), pl.BlockSpec(BLOCK, kept)
    first_spec = pl.BlockSpec(BLOCK, lambda pair, chunk, facts: (0, pair, 0))
    return pl.pallas_call(
        functools.partial(back_kernel, scale, len(pieces), keep),
        grid_spec=pltpu.PrefetchScalarGridSpec(
            num_scalar_prefetch=1,
            grid=(2, 512 // CHUNK),
            in_specs=[spec, first_spec, spec, spec]
            + [pl.BlockSpec(piece.shape, lambda pair, chunk, facts: (0, 0)) for piece in pieces],
            out_specs=[spec, kept_spec, kept_spec] if keep else [spec],
            scratch_shapes=stores(),
        ),
        out_shape=[jax.ShapeDtypeStruct(SHAPE, jnp.bfloat16)]
        + [jax.ShapeDtypeStruct(KEPT_SHAPE, jnp.float32)] * (2 if keep else 0),
        input_output_aliases={2: 0},
        compiler_params=pltpu.CompilerParams(vmem_limit_bytes=52 << 20),
        cost_estimate=estimate(1.0 if keep else 0.25),
        name=name,
    )(facts, queries, out, means, logs, *pieces)


STEP = [(s, s + 1) for s in range(15)]
MIDDLE = [(s // 4) * 4 + (s - 1) % 4 for s in range(14)]
LEG_ONE = [(s, MIDDLE[s]) for s in range(14)]
LEG_TWO = [(MIDDLE[s], s + 2) for s in range(14)]


def body(queries, keys, values, doc_lengths):
    tokens = queries.shape[0]
    scale = math.log2(math.e) / math.sqrt(queries.shape[2])
    kv = jnp.concatenate([keys.reshape(tokens, 512), values.reshape(tokens, 512)], axis=1)
    middle = (tokens + FORWARD) // 32 * 16
    near_low = lax.ppermute(kv[:CUT], "ctx", STEP)
    one_mid = lax.ppermute(kv[FORWARD:middle], "ctx", LEG_ONE)
    near_high = lax.ppermute(kv[CUT:], "ctx", STEP)
    one_high = lax.ppermute(kv[middle:], "ctx", LEG_ONE)

    first = lax.axis_index("ctx") * tokens
    lengths = doc_lengths[0]
    order = jnp.arange(lengths.shape[0])
    ends = jnp.sum(jnp.where(order[:, None] <= order[None, :], lengths[:, None], 0), axis=0)
    position = first + jnp.arange(tokens, dtype=jnp.int32)
    starts = jnp.max(jnp.where(ends[None, :] <= position[:, None], ends[None, :], 0), axis=1)
    allowed = (position[None, :] <= position[:, None]) & (position[None, :] >= starts[:, None])
    bias = jnp.where(allowed, 0.0, NEG).astype(jnp.float32).reshape(tokens, 1, tokens)
    start = jnp.max(jnp.where(ends <= first, ends, 0))
    end = jnp.min(jnp.where(ends > first, ends, jnp.iinfo(jnp.int32).max))
    reach = jnp.minimum(end - first, tokens)
    near_rows = jnp.where(start < first, reach, 0)
    far_rows = jnp.where(start < first - tokens, reach, 0)
    near_facts = jnp.stack([near_rows, jnp.maximum(start - first + tokens, 0), far_rows])
    far_facts = jnp.stack([far_rows, jnp.maximum(start - first + 2 * tokens, 0), far_rows])

    out, means, logs = own_tile(queries, bias, kv, scale)
    far_low = lax.ppermute(near_low[:FORWARD], "ctx", STEP)
    far_mid = lax.ppermute(one_mid, "ctx", LEG_TWO)
    far_high = lax.ppermute(one_high, "ctx", LEG_TWO)
    out, means, logs = back_tile(
        near_facts, queries, out, means, logs, [near_low, near_high], scale, True, "near_tile"
    )
    [out] = back_tile(
        far_facts, queries, out, means, logs, [far_low, far_mid, far_high], scale, False, "far_tile"
    )
    return out


def solution(mesh):
    placed = (
        P(("dp", "ctx"), None, None),
        P(("dp", "ctx"), None, None),
        P(("dp", "ctx"), None, None),
        P("dp", None),
    )
    return jax.shard_map(
        body, mesh=mesh, in_specs=placed, out_specs=P(("dp", "ctx"), None, None), check_vma=False
    )
```
